32 devices in a mesh: dp: 4 (over y, x), seq: 8 (over z, core).
Axes of the slice: x: 2, y: 2, z: 4, core: 2. Of those that a mesh axis runs over, the one named last changes fastest.
Arguments:
- inputs: float32 [4, 4096, 1024], P('dp', 'seq'), may hold values from -6 to 6
- norm_gain: bfloat16 [2, 1024], P(None, 'dp'), may hold values from 0.25 to 1.75
- in_weight: bfloat16 [2, 1024, 4384], P(None, 'dp'), may hold values from -0.1875 to 0.1875
- conv_weight: bfloat16 [2, 4, 2304], P(None, None, 'dp'), may hold values from -3 to 3
- conv_bias: bfloat16 [2, 2304], P(None, 'dp'), may hold values from -0.5 to 0.5
- dt_bias: bfloat16 [2, 32], P(None, 'dp'), may hold values from -6 to 0.5
- a_log: bfloat16 [2, 32], P(None, 'dp'), may hold values from -4 to 1
- skip_gain: bfloat16 [2, 32], P(None, 'dp'), may hold values from 0.5 to 2
- gate_gain: bfloat16 [2, 2048], P(None, 'dp'), may hold values from 0.25 to 1.75
- out_weight: bfloat16 [2, 2048, 1024], P(None, 'dp'), may hold values from -0.125 to 0.125
- cotangent: float32 [4, 4096, 1024], P('dp', 'seq'), may hold values from -6 to 6
Outputs:
- output: float32 [4, 4096, 1024], P('dp', 'seq')
- input_grad: float32 [4, 4096, 1024], P('dp', 'seq')
- grad_norm_gain: float32 [2, 1024], P(None, 'dp')
- grad_in_weight: float32 [2, 1024, 4384], P(None, 'dp')
- grad_conv_weight: float32 [2, 4, 2304], P(None, None, 'dp')
- grad_conv_bias: float32 [2, 2304], P(None, 'dp')
- grad_dt_bias: float32 [2, 32], P(None, 'dp')
- grad_a_log: float32 [2, 32], P(None, 'dp')
- grad_skip_gain: float32 [2, 32], P(None, 'dp')
- grad_gate_gain: float32 [2, 2048], P(None, 'dp')
- grad_out_weight: float32 [2, 2048, 1024], P(None, 'dp')
The draws below stay inside these ranges and needn't reach their ends.
All inputs are finite; a program needn't handle non-finite values.
Results may differ from the reference program's by a relative error of at most 0.02.
Values may be sent and summed in bfloat16 or wider, within the bound.
A program may use at most 320 MiB of HBM per device.

```python
import jax
import jax.numpy as jnp
from jax import lax

D = 1024
HEADS = 32
HEAD_DIM = 64
STATE = 128
CONV = 4
GROUP = 256
LAYERS = 2
INNER = 2048
XBC = 2304
PROJ = 4384
LENGTH = 4096
SEQS = 4


def level_of(rng, extent, cuts, least, largest):
    level, own = 1.0, jax.random.fold_in(rng, 6)
    for dim, parts in cuts:
        steps = jnp.exp(jax.random.uniform(jax.random.fold_in(own, dim), (parts,), jnp.float32, least / len(cuts), largest / len(cuts)))
        level = level * jnp.repeat(steps, extent[dim] // parts).reshape([-1 if axis == dim else 1 for axis in range(len(extent))])
    return level


def bell_draw(stream_key, dims, scale, most, cuts=(), dtype=jnp.bfloat16):
    level = level_of(stream_key, dims, cuts, -0.22, 0.18) if cuts else 1.0
    values = jax.random.normal(stream_key, dims, jnp.float32) * scale * level
    return jnp.minimum(jnp.maximum(values, -most), most).astype(dtype)


def setup_inputs(seed: int = 0) -> dict:
    key_list = jax.random.split(jax.random.key(seed), 12)
    return {
        "inputs": bell_draw(key_list[0], (SEQS, LENGTH, D), 1.0, 6.0, ((0, 4), (1, 8)), jnp.float32),
        "norm_gain": jnp.clip(1.0 + 0.15 * jax.random.normal(key_list[1], (LAYERS, D), jnp.float32), 0.25, 1.75).astype(jnp.bfloat16),
        "in_weight": bell_draw(key_list[2], (LAYERS, D, PROJ), D ** -0.5, 0.1875, ((1, 4),)),
        "conv_weight": bell_draw(key_list[3], (LAYERS, CONV, XBC), CONV ** -0.5, 3.0, ((2, 4),)),
        "conv_bias": jnp.clip(jax.random.uniform(key_list[4], (LAYERS, XBC), jnp.float32, -0.5, 0.5) * level_of(key_list[4], (LAYERS, XBC), ((1, 4),), -0.4, 0.0), -0.5, 0.5).astype(jnp.bfloat16),
        "dt_bias": jnp.clip(-6.0 + 6.5 * jax.random.uniform(key_list[5], (LAYERS, HEADS), jnp.float32) ** level_of(key_list[5], (LAYERS, HEADS), ((1, 4),), -0.2, 0.2), -6.0, 0.5).astype(jnp.bfloat16),
        "a_log": jnp.clip(-4.0 + 5.0 * jax.random.uniform(key_list[6], (LAYERS, HEADS), jnp.float32) ** level_of(key_list[6], (LAYERS, HEADS), ((1, 4),), -0.2, 0.2), -4.0, 1.0).astype(jnp.bfloat16),
        "skip_gain": jnp.clip(0.5 + 1.5 * jax.random.uniform(key_list[7], (LAYERS, HEADS), jnp.float32) ** level_of(key_list[7], (LAYERS, HEADS), ((1, 4),), -0.2, 0.2), 0.5, 2.0).astype(jnp.bfloat16),
        "gate_gain": jnp.clip(1.0 + 0.15 * jax.random.normal(key_list[8], (LAYERS, INNER), jnp.float32), 0.25, 1.75).astype(jnp.bfloat16),
        "out_weight": bell_draw(key_list[9], (LAYERS, INNER, D), INNER ** -0.5, 0.125, ((1, 4),)),
        "cotangent": bell_draw(key_list[10], (SEQS, LENGTH, D), 1.0, 6.0, ((0, 4), (1, 8)), jnp.float32),
    }


@jax.custom_vjp
def low(v):
    return lax.optimization_barrier(v.astype(jnp.bfloat16)).astype(jnp.float32)

@jax.custom_vjp
def low_back(v):
    return v

def low_keep(v):
    return (low(v), None)

def low_pass(kept, grad):
    return (grad,)

def back_keep(v):
    return (v, None)

def back_low(kept, grad):
    return (low(grad),)
low.defvjp(low_keep, low_pass)
low_back.defvjp(back_keep, back_low)
epsilon = 1e-05
highest = lax.Precision.HIGHEST

def rms_norm(values, gain):
    return values * lax.rsqrt(lax.optimization_barrier(jnp.mean(values * values, axis=-1, keepdims=True)) + epsilon) * gain

def wide_dot(left, right):
    return jnp.dot(left, right, precision=highest, preferred_element_type=jnp.float32)

def group_step(carried, pieces):
    values, step_size, log_decay, b_mat, c_mat = pieces
    group_sum = jnp.cumsum(log_decay, axis=0)
    by_head = group_sum.T
    causal = jnp.arange(GROUP)[:, None] >= jnp.arange(GROUP)[None, :]
    decays = jnp.exp(jnp.where(causal[None], by_head[:, :, None] - by_head[:, None, :], -jnp.inf))
    scores = wide_dot(c_mat, b_mat.T)
    scaled = values * step_size[:, :, None]
    within = jnp.einsum('hij,jhp->ihp', decays * scores[None], scaled, precision=highest)
    from_state = jnp.exp(group_sum)[:, :, None] * jnp.einsum('in,hpn->ihp', c_mat, carried, precision=highest)
    tails = jnp.exp(group_sum[-1][None, :] - group_sum)
    updated = jnp.exp(group_sum[-1])[:, None, None] * carried + jnp.einsum('jhp,jn->hpn', scaled * tails[:, :, None], b_mat, precision=highest)
    return (updated, within + from_state)

def mixer_block(hidden, params):
    norm_gain, in_weight, conv_weight, conv_bias, dt_bias, a_log, skip_gain, gate_gain, out_weight = params
    length = hidden.shape[0]
    blocks = length // GROUP
    normed = rms_norm(hidden, norm_gain)
    projected = low_back(wide_dot(low(normed), in_weight))
    gate_z = projected[:, :INNER]
    conv_in = low(projected[:, INNER:INNER + XBC])
    dt_raw = projected[:, INNER + XBC:]
    padded = jnp.concatenate([jnp.zeros((CONV - 1, XBC), jnp.float32), conv_in], axis=0)
    conv_out = conv_bias + jnp.zeros((length, XBC), jnp.float32)
    for tap_idx in range(CONV):
        conv_out = conv_out + conv_weight[tap_idx] * padded[tap_idx:tap_idx + length]
    conv_out = low_back(conv_out)
    active = jax.nn.silu(conv_out)
    values = active[:, :INNER].reshape(length, HEADS, HEAD_DIM)
    b_mat = active[:, INNER:INNER + STATE]
    c_mat = active[:, INNER + STATE:]
    step_size = jax.nn.softplus(dt_raw + dt_bias)
    log_decay = step_size * -jnp.exp(a_log)
    pieces = (values.reshape(blocks, GROUP, HEADS, HEAD_DIM), step_size.reshape(blocks, GROUP, HEADS), log_decay.reshape(blocks, GROUP, HEADS), b_mat.reshape(blocks, GROUP, STATE), c_mat.reshape(blocks, GROUP, STATE))
    start_state = jnp.zeros((HEADS, HEAD_DIM, STATE), jnp.float32)
    final_state, ssm_out = lax.scan(jax.checkpoint(group_step), start_state, pieces)
    mixed = ssm_out.reshape(length, HEADS, HEAD_DIM) + skip_gain[:, None] * values
    gated = mixed.reshape(length, INNER) * jax.nn.silu(gate_z)
    normed_out = rms_norm(gated, gate_gain)
    branch = low_back(wide_dot(low(normed_out), out_weight))
    return hidden + branch

def reference(inputs, norm_gain, in_weight, conv_weight, conv_bias, dt_bias, a_log, skip_gain, gate_gain, out_weight, cotangent):
    params = (norm_gain.astype(jnp.float32), in_weight.astype(jnp.float32), conv_weight.astype(jnp.float32), conv_bias.astype(jnp.float32), dt_bias.astype(jnp.float32), a_log.astype(jnp.float32), skip_gain.astype(jnp.float32), gate_gain.astype(jnp.float32), out_weight.astype(jnp.float32))

    def whole(all_inputs, all_params):

        def one_sequence(seq_inputs):
            hidden = seq_inputs
            for layer_idx in range(LAYERS):
                hidden = mixer_block(hidden, tuple((member[layer_idx] for member in all_params)))
            return hidden
        return lax.map(one_sequence, all_inputs)
    result, pullback = jax.vjp(whole, inputs.astype(jnp.float32), params)
    grad_inputs, grad_params = pullback(cotangent.astype(jnp.float32))
    return (result, grad_inputs, grad_params[0], grad_params[1], grad_params[2], grad_params[3], grad_params[4], grad_params[5], grad_params[6], grad_params[7], grad_params[8])
```

```python
import functools

import jax
import jax.numpy as jnp
from jax import lax
from jax.experimental import pallas as pl
from jax.experimental.pallas import tpu as pltpu
from jax.sharding import PartitionSpec as P

HEADS = 32
HEAD_DIM = 64
STATE = 128
GROUP = 256
INNER = 2048
XBC = 2304
CHUNKS = 8


epsilon = 1e-05
highest = lax.Precision.HIGHEST
plain = lax.Precision.DEFAULT


def passed_along(value, axis, steps):
    count = lax.axis_size(axis)
    first, last = (max(0, -steps), min(count, count - steps))
    return lax.ppermute(value, axis, [(source, source + steps) for source in range(first, last)])


def rms_norm(values, gain):
    return values * lax.rsqrt(jnp.mean(values * values, axis=-1, keepdims=True) + epsilon) * gain


def chain_kernel(count, step, decay_ref, local_ref, out_ref, send, held, send_sem, recv_sem):
    me = lax.axis_index("seq")
    place = me if step > 0 else count - 1 - me
    has_source = place > 0
    has_target = place < count - 1
    barrier = pltpu.get_barrier_semaphore()

    @pl.when(has_source)
    def _():
        pl.semaphore_signal(
            barrier, inc=1, device_id={"seq": me - step}, device_id_type=pl.DeviceIdType.MESH
        )

    @pl.when(has_target)
    def _():
        pl.semaphore_wait(barrier, 1)

    width = out_ref.shape[0] // CHUNKS

    def copy_of(chunk):
        return pltpu.make_async_remote_copy(
            src_ref=send.at[chunk],
            dst_ref=held.at[chunk],
            send_sem=send_sem.at[chunk],
            recv_sem=recv_sem.at[chunk],
            device_id={"seq": me + step},
            device_id_type=pl.DeviceIdType.MESH,
        )

    for chunk in range(CHUNKS):
        part = pl.ds(chunk * width, width)

        @pl.when(has_source)
        def _():
            copy_of(chunk).wait_recv()
            out_ref[part] = held[chunk].astype(jnp.float32)

        @pl.when(jnp.logical_not(has_source))
        def _():
            out_ref[part] = jnp.zeros((width,) + out_ref.shape[1:], jnp.float32)

        @pl.when(has_target)
        def _():
            send[chunk] = (decay_ref[part] * out_ref[part] + local_ref[part]).astype(jnp.bfloat16)
            copy_of(chunk).start()

    @pl.when(has_target)
    def _():
        for chunk in range(CHUNKS):
            copy_of(chunk).wait_send()


def chain(decay, local, step):
    count = lax.axis_size("seq")
    shape = (HEADS, HEAD_DIM, STATE)
    pieces = (CHUNKS, HEADS // CHUNKS, HEAD_DIM, STATE)
    return pl.pallas_call(
        functools.partial(chain_kernel, count, step),
        out_shape=jax.ShapeDtypeStruct(shape, jnp.float32),
        in_specs=[pl.BlockSpec(memory_space=pltpu.VMEM)] * 2,
        out_specs=pl.BlockSpec(memory_space=pltpu.VMEM),
        scratch_shapes=[
            pltpu.VMEM(pieces, jnp.bfloat16),
            pltpu.VMEM(pieces, jnp.bfloat16),
            pltpu.SemaphoreType.DMA((CHUNKS,)),
            pltpu.SemaphoreType.DMA((CHUNKS,)),
        ],
        cost_estimate=pl.CostEstimate(flops=2**20, bytes_accessed=2**25, transcendentals=0),
        compiler_params=pltpu.CompilerParams(
            collective_id=0 if step > 0 else 1,
            has_side_effects=True,
            vmem_limit_bytes=16 * 2**20,
        ),
    )(jnp.broadcast_to(decay[:, None, None], (HEADS, 1, STATE)), local)


def conv_apply(extended, conv_weight, conv_bias, length):
    total = conv_bias + jnp.zeros((length, conv_bias.shape[0]), jnp.float32)
    for tap_idx in range(conv_weight.shape[0]):
        total = total + conv_weight[tap_idx] * extended[tap_idx : tap_idx + length].astype(
            jnp.float32
        )
    return total


def shard_parts(conv_out, dt_raw, dt_bias, a_log):
    length = conv_out.shape[0]
    blocks = length // GROUP
    active = jax.nn.silu(conv_out)
    values = active[:, :INNER].reshape(blocks, GROUP, HEADS, HEAD_DIM)
    b_mat = active[:, INNER : INNER + STATE].reshape(blocks, GROUP, STATE)
    c_mat = active[:, INNER + STATE :].reshape(blocks, GROUP, STATE)
    step_size = jax.nn.softplus(dt_raw + dt_bias)
    log_decay = (step_size * -jnp.exp(a_log)).reshape(blocks, GROUP, HEADS)
    causal = lax.broadcasted_iota(jnp.int32, (GROUP, GROUP), 0) >= lax.broadcasted_iota(
        jnp.int32, (GROUP, GROUP), 1
    )
    group_sum = jnp.einsum("ij,kjh->kih", causal.astype(jnp.float32), log_decay, precision=highest)
    scaled = values * step_size.reshape(blocks, GROUP, HEADS)[:, :, :, None]
    tails = jnp.exp(group_sum[:, -1:, :] - group_sum)
    group_states = jnp.einsum(
        "kjhp,kjn->khpn", scaled * tails[:, :, :, None], b_mat, precision=plain
    )
    group_decay = jnp.exp(group_sum[:, -1, :])
    return values, b_mat, c_mat, group_sum, scaled, group_states, group_decay, causal


def run_states(start, group_states, group_decay):
    entering, running = [], start
    for block_idx in range(group_states.shape[0]):
        entering.append(running)
        running = group_decay[block_idx][:, None, None] * running + group_states[block_idx]
    return jnp.stack(entering), running


def shard_scan(conv_out, dt_raw, dt_bias, a_log, skip_gain, incoming):
    length = conv_out.shape[0]
    values, b_mat, c_mat, group_sum, scaled, group_states, group_decay, causal = shard_parts(
        conv_out, dt_raw, dt_bias, a_log
    )
    by_head = jnp.swapaxes(group_sum, 1, 2)
    decays = jnp.exp(jnp.where(causal, by_head[:, :, :, None] - by_head[:, :, None, :], -jnp.inf))
    scores = jnp.einsum("kin,kjn->kij", c_mat, b_mat, precision=plain)
    within = jnp.einsum("khij,kjhp->kihp", decays * scores[:, None], scaled, precision=plain)
    entering, final = run_states(incoming, group_states, group_decay)
    carried = jnp.einsum("kin,khpn->kihp", c_mat, entering, precision=plain)
    mixed = (
        within + jnp.exp(group_sum)[:, :, :, None] * carried + skip_gain[:, None] * values
    )
    return mixed.reshape(length, INNER), final


def finish(mixed, gate_z, gate_gain):
    return rms_norm(mixed * jax.nn.silu(gate_z), gate_gain)


SMALL = (0, 2, 3, 4, 5, 6, 7)


def body(
    inputs,
    norm_gain,
    in_weight,
    conv_weight,
    conv_bias,
    dt_bias,
    a_log,
    skip_gain,
    gate_gain,
    out_weight,
    cotangent,
):
    layers = in_weight.shape[0]
    hidden = inputs[0]
    length = hidden.shape[0]
    taps = conv_weight.shape[1]
    rim_rows = taps - 1
    owners = lax.axis_size("dp")

    small = (norm_gain, conv_weight, conv_bias, dt_bias, a_log, skip_gain, gate_gain)
    extents = [member.reshape(layers, -1).shape[1] for member in small]
    starts = [sum(extents[:idx]) for idx in range(len(extents) + 1)]
    packed = jnp.concatenate([member.reshape(layers, -1) for member in small], axis=1)
    packed = lax.all_gather(packed.reshape(-1), "dp").astype(jnp.float32)
    packed = packed.reshape(owners, layers, -1)

    def small_of(layer_idx, member_idx):
        own = packed[:, layer_idx, starts[member_idx] : starts[member_idx + 1]]
        if member_idx != 1:
            return own.reshape(-1)
        return jnp.swapaxes(own.reshape(owners, taps, -1), 0, 1).reshape(taps, -1)

    def gather(shard):
        return lax.all_gather(shard, "dp", axis=0, tiled=True)

    saved = []
    for layer_idx in range(layers):
        gains = [small_of(layer_idx, member_idx) for member_idx in range(len(small))]
        conv_proj = gather(in_weight[layer_idx][:, INNER:])
        gate_proj = gather(in_weight[layer_idx][:, :INNER])
        out_proj = gather(out_weight[layer_idx])
        normed_low = rms_norm(hidden, gains[0]).astype(jnp.bfloat16)
        projected = jnp.dot(normed_low, conv_proj, preferred_element_type=jnp.float32)
        conv_in = projected[:, :XBC].astype(jnp.bfloat16)
        dt_raw = projected[:, XBC:]
        arrived = passed_along(conv_in[length - rim_rows :], "seq", 1)
        extended = jnp.concatenate([arrived, conv_in], axis=0)
        conv_out = conv_apply(extended, gains[1], gains[2], length)
        parts = shard_parts(conv_out, dt_raw, gains[3], gains[4])
        group_states, group_decay = parts[5], parts[6]
        local_state = run_states(
            jnp.zeros((HEADS, HEAD_DIM, STATE), jnp.float32), group_states, group_decay
        )[1]
        shard_decay = jnp.prod(group_decay, axis=0)
        incoming = chain(shard_decay, local_state, 1)
        gate_z = jnp.dot(normed_low, gate_proj, preferred_element_type=jnp.float32)
        (mixed, _), scan_pull = jax.vjp(
            lambda *args: shard_scan(*args, incoming),
            conv_out,
            dt_raw,
            gains[3],
            gains[4],
            gains[5],
        )
        normed_out, finish_pull = jax.vjp(finish, mixed, gate_z, gains[6])
        low_out = normed_out.astype(jnp.bfloat16)
        branch = jnp.dot(low_out, out_proj, preferred_element_type=jnp.float32)
        saved.append(
            (
                hidden,
                normed_low,
                extended,
                parts[2],
                parts[3],
                group_decay,
                shard_decay,
                low_out,
                scan_pull,
                finish_pull,
                gains,
                (conv_proj, gate_proj, out_proj),
            )
        )
        hidden = hidden + branch

    last_sum = [None]

    def summed(grad):
        part = lax.psum_scatter(
            grad.astype(jnp.bfloat16), "dp", scatter_dimension=0, tiled=True
        )
        if last_sum[0] is not None:
            part, _ = lax.optimization_barrier((part, last_sum[0]))
        last_sum[0] = lax.psum(part, "seq")
        return last_sum[0]

    def outer(left, right):
        return lax.dot_general(
            left, right, (((0,), (0,)), ((), ())), preferred_element_type=jnp.float32
        )

    def times_transposed(left, right):
        return lax.dot_general(
            left, right, (((1,), (1,)), ((), ())), preferred_element_type=jnp.float32
        )

    grad_hidden = cotangent[0]
    grad_in, grad_out, grad_small = [None] * layers, [None] * layers, [None] * layers
    for layer_idx in reversed(range(layers)):
        (
            hidden_in,
            normed_low,
            extended,
            c_mat,
            group_sum,
            group_decay,
            shard_decay,
            low_out,
            scan_pull,
            finish_pull,
            gains,
            (conv_proj, gate_proj, out_proj),
        ) = saved[layer_idx]
        blocks = length // GROUP
        grad_branch = grad_hidden.astype(jnp.bfloat16)
        grad_out[layer_idx] = summed(outer(low_out, grad_branch))
        grad_mixed, grad_gate_z, grad_gate_gain = finish_pull(
            times_transposed(grad_branch, out_proj)
        )
        by_block = grad_mixed.reshape(blocks, GROUP, HEADS, HEAD_DIM)
        entering_grads = jnp.einsum(
            "kihp,kin->khpn",
            jnp.exp(group_sum)[:, :, :, None] * by_block,
            c_mat,
            precision=plain,
        )
        direct = jnp.zeros_like(entering_grads[0])
        for block_idx in reversed(range(blocks)):
            direct = group_decay[block_idx][:, None, None] * direct + entering_grads[block_idx]
        state_grad = chain(shard_decay, direct, -1)
        gate_low = grad_gate_z.astype(jnp.bfloat16)
        grad_in_gate = summed(outer(normed_low, gate_low))
        grad_conv_out, grad_dt_raw, grad_dt_bias, grad_a_log, grad_skip = scan_pull(
            (grad_mixed, state_grad)
        )
        conv_grad = grad_conv_out.astype(jnp.bfloat16).astype(jnp.float32)
        extended_wide = extended.astype(jnp.float32)
        grad_conv_weight = jnp.stack(
            [
                jnp.sum(conv_grad * extended_wide[tap_idx : tap_idx + length], axis=0)
                for tap_idx in range(taps)
            ]
        )
        grad_conv_bias = jnp.sum(conv_grad, axis=0)
        grad_extended = jnp.zeros((length + rim_rows, conv_grad.shape[1]), jnp.float32)
        for tap_idx in range(taps):
            grad_extended = grad_extended + jnp.pad(
                gains[1][tap_idx] * conv_grad, ((tap_idx, rim_rows - tap_idx), (0, 0))
            )
        returned = passed_along(grad_extended[:rim_rows], "seq", -1)
        grad_conv_in = grad_extended[rim_rows:] + jnp.pad(
            returned, ((length - rim_rows, 0), (0, 0))
        )
        conv_low = jnp.concatenate([grad_conv_in, grad_dt_raw], axis=1).astype(jnp.bfloat16)
        grad_in[layer_idx] = (grad_in_gate, summed(outer(normed_low, conv_low)))
        grad_normed = times_transposed(gate_low, gate_proj) + times_transposed(
            conv_low, conv_proj
        )
        _, norm_pull = jax.vjp(rms_norm, hidden_in, gains[0])
        grad_input_part, grad_norm_gain = norm_pull(grad_normed)
        grad_hidden = grad_hidden + grad_input_part
        by_owner = [
            grad.reshape(owners, -1)
            for grad in (
                grad_norm_gain,
                jnp.swapaxes(grad_conv_weight.reshape(taps, owners, -1), 0, 1),
                grad_conv_bias,
                grad_dt_bias,
                grad_a_log,
                grad_skip,
                grad_gate_gain,
            )
        ]
        grad_small[layer_idx] = jnp.concatenate(by_owner, axis=1)
    totals = lax.psum(jnp.stack(grad_small, axis=1), ("dp", "seq"))
    mine = lax.dynamic_index_in_dim(totals, lax.axis_index("dp"), 0, keepdims=False)
    owned = [
        mine[:, starts[idx] : starts[idx + 1]].reshape(member.shape)
        for idx, member in enumerate(small)
    ]
    in_total = jnp.stack(
        [jnp.concatenate(pieces, axis=1).astype(jnp.float32) for pieces in grad_in]
    )
    out_total = jnp.stack([piece.astype(jnp.float32) for piece in grad_out])
    return (
        hidden[None],
        grad_hidden[None],
        owned[0],
        in_total,
        owned[1],
        owned[2],
        owned[3],
        owned[4],
        owned[5],
        owned[6],
        out_total,
    )


def solution(mesh):
    in_specs = (
        P("dp", "seq", None),
        P(None, "dp"),
        P(None, "dp", None),
        P(None, None, "dp"),
        P(None, "dp"),
        P(None, "dp"),
        P(None, "dp"),
        P(None, "dp"),
        P(None, "dp"),
        P(None, "dp", None),
        P("dp", "seq", None),
    )
    out_specs = (
        P("dp", "seq", None),
        P("dp", "seq", None),
        P(None, "dp"),
        P(None, "dp", None),
        P(None, None, "dp"),
        P(None, "dp"),
        P(None, "dp"),
        P(None, "dp"),
        P(None, "dp"),
        P(None, "dp"),
        P(None, "dp", None),
    )
    return jax.shard_map(body, mesh=mesh, in_specs=in_specs, out_specs=out_specs, check_vma=False)
```
